32 devices in a mesh: section: 4 (over y, x), expert: 8 (over z, core).
Axes of the slice: x: 2, y: 2, z: 4, core: 2. Of those that a mesh axis runs over, the one named last changes fastest.
Arguments:
- state: bfloat16 [2, 4, 512, 2048], P(None, 'section', 'expert'), may hold values from -6 to 6
- norm_gain: float32 [2, 4, 2048], P(None, 'section'), may hold values from 0.1 to 1.9
- up_weight: bfloat16 [2, 4, 8, 2048, 768], P(None, 'section', 'expert'), may hold values from -0.125 to 0.125
- down_weight: bfloat16 [2, 4, 8, 768, 2048], P(None, 'section', 'expert'), may hold values from -0.21875 to 0.21875
- expert_ids: int32 [4, 2, 4, 512, 2], P(None, None, 'section'), may hold values from 0 to 7, all different within a row; in each aligned block of 64 rows (0 to 63, 64 to 127, ..., all dimensions but the last counted through in order) at most 32 rows name the same one
- gate_values: float32 [4, 2, 4, 512, 2], P(None, None, 'section', 'expert'), may hold values from 0.1 to 1
Outputs:
- final_state: bfloat16 [2, 4, 512, 2048], P(None, 'section', 'expert')
- finished: bfloat16 [4, 512, 2048], P(None, 'expert', 'section')
The draws below stay inside these ranges and needn't reach their ends.
Inputs may be any that keep to these rules, and one draw needn't show every extreme that they name: `expert_ids`: each token names two different experts. Within the 64 tokens of one index of expert (aligned blocks of 64 tokens) at one tick, slot and segment, no expert is named more than 32 times.
All inputs are finite; a program needn't handle non-finite values.
Results may differ from the reference program's by a relative error of at most 0.0095.
Values may be sent and summed in bfloat16 or wider, within the bound.
A program may use at most 64 MiB of HBM per device.

```python
import math
import jax
import jax.numpy as jnp
import numpy as np
from jax import lax

D = 2048
FF = 768
TICKS = 4
TOK_DEV = 64
TOK = 512
MOST = 32
EXPERTS = 8
N_SECTION = 4
N_EXPERT = 8


def block_levels(stream_key, dims, cuts, low, top_value):
    loudness = 1.0
    for position, blocks in cuts:
        draws = jax.random.uniform(jax.random.fold_in(jax.random.fold_in(stream_key, 6), position), (blocks,), jnp.float32, low / len(cuts), top_value / len(cuts))
        loudness = loudness * jnp.repeat(jnp.exp(draws), dims[position] // blocks).reshape((-1,) + (1,) * (len(dims) - 1 - position))
    return loudness


def routed_block(stream_key, own, number, rows, count, top, reach, lean):
    order = jax.random.permutation(stream_key, count)
    heavy_load, common = load_shares(count, rows * top, reach, lean, True), load_shares(count, rows * top, reach, lean, False)
    places = jnp.arange(count)

    def named(tallies, offset_by):
        used = int((tallies > 0).sum())
        fixed = max(1, used // 4)
        passed = fixed + (places - fixed + offset_by * (used - fixed)) % max(1, count - fixed)
        return jnp.zeros((count,), jnp.int32).at[order[jnp.where(places < fixed, places, passed)]].set(jnp.asarray(tallies, jnp.int32))

    tallies = jnp.where(number % 4 == 0, named(heavy_load, number // 4), named(common, number - number // 4 - 1))
    mixed = jax.random.permutation(jax.random.fold_in(own, 3), count)
    giver, receiver = mixed[0:count // 2 * 2:2], mixed[1:count // 2 * 2:2]
    margin = jnp.minimum(tallies[giver] - 1, reach - tallies[receiver]) // 2
    margin = jnp.where((giver == order[0]) | (receiver == order[0]) | (tallies[receiver] == 0), 0, jnp.maximum(margin, 0))
    passed = jax.random.randint(jax.random.fold_in(own, 4), (count // 2,), 0, 1 << 20) % (margin + 1)
    tallies = tallies.at[giver].add(-passed).at[receiver].add(passed)
    labels = jnp.searchsorted(jnp.cumsum(tallies), jnp.arange(rows * top), side="right").astype(jnp.int32)
    listing = labels.reshape(top, rows).T
    listing = listing[jax.random.permutation(jax.random.fold_in(own, 1), rows)]
    offset_by = jax.random.randint(jax.random.fold_in(own, 2), (rows, 1), 0, top)
    return jnp.take_along_axis(listing, (jnp.arange(top)[None, :] + offset_by) % top, axis=1)


def load_shares(amount, total, limit, skew, full):
    weights = [(1 << 20) // math.isqrt(grade ** skew) + 1 for grade in range(1, amount + 1)]
    largest = limit if full else min(limit, max(-(-total // amount), total * weights[0] // sum(weights)))
    least = 1 if total - largest >= amount - 1 else 0
    counts, surplus = [largest] + [least] * (amount - 1), total - largest - least * (amount - 1)
    while surplus > 0:
        movable = [i for i in range(1, amount) if counts[i] < largest] or [i for i in range(1, amount) if counts[i] < limit]
        whole, remaining = sum([weights[i] for i in movable]), surplus
        for i in movable:
            extra = min(limit - counts[i], max(1, remaining * weights[i] // whole), surplus)
            counts[i] = counts[i] + extra
            surplus = surplus - extra
    return np.array(counts)


def centred(rng, dims, spread, bound, split=(), kind=jnp.bfloat16):
    gain = block_levels(rng, dims, split, -0.22, 0.18) if split else 1.0
    array = jax.random.normal(rng, dims, jnp.float32) * spread * gain
    return jnp.minimum(jnp.maximum(array, -bound), bound).astype(kind)


def setup_inputs(seed: int = 0) -> dict:
    seeds = jax.random.split(jax.random.key(seed), 7)
    state = centred(seeds[0], (2, N_SECTION, TOK, D), 1.0, 6.0, ((1, 4), (2, 8)))
    norm_gain = jnp.clip(1.0 + 0.18 * jax.random.normal(seeds[1], (2, N_SECTION, D), jnp.float32), 0.1, 1.9)
    up_weight = centred(seeds[2], (2, N_SECTION, EXPERTS, D, FF), D ** -0.5, 0.125, ((1, 4), (2, 8)))
    down_weight = centred(seeds[3], (2, N_SECTION, EXPERTS, FF, D), FF ** -0.5, 0.21875, ((1, 4), (2, 8)))
    expert_ids_keys = jax.random.split(jax.random.fold_in(seeds[4], 1), TICKS * 2 * N_SECTION * TOK // TOK_DEV)
    expert_ids_turns = jax.random.permutation(jax.random.fold_in(seeds[4], 3), TICKS * 2 * N_SECTION * TOK // TOK_DEV)
    expert_ids = jax.vmap(lambda own, number: routed_block(jax.random.fold_in(seeds[4], 2), own, number, TOK_DEV, EXPERTS, 2, MOST, 2))(expert_ids_keys, expert_ids_turns).reshape((TICKS, 2, N_SECTION, TOK, 2))
    gate_values = jnp.clip(0.1 + 0.9 * jax.random.uniform(seeds[5], (TICKS, 2, N_SECTION, TOK, 2), jnp.float32) ** block_levels(seeds[5], (TICKS, 2, N_SECTION, TOK, 2), ((2, 4), (3, 8)), -0.2, 0.2), 0.1, 1.0)
    return {"state": state, "norm_gain": norm_gain, "up_weight": up_weight, "down_weight": down_weight, "expert_ids": expert_ids, "gate_values": gate_values}


def rms_norm(layer_in, norm_gain):
    widened = layer_in.astype(jnp.float32)
    scaled = lax.rsqrt(lax.optimization_barrier(jnp.mean(widened * widened, axis=-1, keepdims=True)) + 1e-06)
    return (widened * scaled * norm_gain).astype(jnp.bfloat16)

def moe_layer(layer_in, norm_gain, up_weight, down_weight, routes, gates):
    normed = rms_norm(layer_in, norm_gain)
    capacity = N_EXPERT * MOST
    all_tokens = layer_in.shape[0]

    def one_expert(accumulated, expert_index):
        matches = routes == expert_index
        token_hit = jnp.any(matches, axis=1)
        weight = lax.optimization_barrier(jnp.sum(jnp.where(matches, gates, 0.0), axis=1))
        row_index = jnp.nonzero(token_hit, size=capacity, fill_value=0)[0].astype(jnp.int32)
        live_count = jnp.sum(token_hit.astype(jnp.int32))
        is_valid = jnp.arange(capacity, dtype=jnp.int32) < live_count
        in_rows = normed[row_index]
        projected = jnp.dot(in_rows, up_weight[expert_index], preferred_element_type=jnp.float32)
        activated = jax.nn.silu(projected).astype(jnp.bfloat16)
        outputs = jnp.dot(activated, down_weight[expert_index], preferred_element_type=jnp.float32).astype(jnp.bfloat16)
        scaled = jnp.where(is_valid, weight[row_index], 0.0)[:, None] * outputs.astype(jnp.float32)
        return (accumulated.at[row_index].add(scaled), None)
    start_sum = jnp.zeros((all_tokens, layer_in.shape[1]), jnp.float32)
    expert_list = jnp.arange(up_weight.shape[0], dtype=jnp.int32)
    accumulated, _ = lax.scan(one_expert, start_sum, expert_list)
    return (layer_in.astype(jnp.float32) + accumulated).astype(jnp.bfloat16)

def apply_segment(packed):
    return moe_layer(packed[0], packed[1], packed[2], packed[3], packed[4], packed[5])

def reference(state, norm_gain, up_weight, down_weight, expert_ids, gate_values):
    current = state
    done_list = []
    for tick_index in range(TICKS):
        results = []
        for group_index in range(2):
            packed = (current[group_index], norm_gain[group_index], up_weight[group_index], down_weight[group_index], expert_ids[tick_index, group_index], gate_values[tick_index, group_index])
            results.append(lax.map(apply_segment, packed))
        first_slot, second_slot = results
        new_first = jnp.concatenate([jnp.zeros_like(first_slot[:1]), first_slot[:-1]], axis=0)
        new_second = jnp.concatenate([first_slot[-1:], second_slot[:-1]], axis=0)
        done_list.append(second_slot[-1])
        current = jnp.stack([new_first, new_second])
    return (current, jnp.stack(done_list))
```

```python
import functools

import jax
import jax.numpy as jnp
from jax import lax
from jax.experimental import pallas as pl
from jax.experimental.pallas import tpu as pltpu
from jax.sharding import PartitionSpec as P

EPS = 1e-06
LANES = 128
VMEM_LIMIT = 60 * 1024 * 1024
VMEM_BUDGET = 44 * 1024 * 1024
MESH = pl.DeviceIdType.MESH


def relay_kernel(
    tick_count, chips, sections, rows, tile,
    state_ref, gain_ref, up_hbm, down_hbm, ids_ref, gates_ref,
    final_ref, finished_ref,
    up, down, layer_in, gathered, partial, from_pair, chain, result, act, row_gate, all_gates,
    load_sem, gate_send, gate_recv,
    line_send, line_recv, share_send, share_recv,
    pair_send, pair_recv, chain_send, chain_recv,
    hop_send, hop_recv, done_send, done_recv, done_local,
):
    width = layer_in.shape[3]
    hidden = up.shape[2]
    experts = 2 * chips
    me = lax.axis_index("expert")
    place = lax.axis_index("section")
    chip, core = me // 2, me % 2
    pair = chip * 2 + 1 - core
    last = sections - 1
    columns = width // sections

    loads = [pltpu.make_async_copy(up_hbm.at[c], up.at[c], load_sem.at[c]) for c in range(2)]
    loads += [pltpu.make_async_copy(down_hbm.at[c], down.at[c], load_sem.at[2 + c]) for c in range(2)]
    for load in loads:
        load.start()

    barrier = pltpu.get_barrier_semaphore()
    for other in range(1, experts):
        pl.semaphore_signal(
            barrier, inc=1, device_id={"expert": (me + other) % experts}, device_id_type=MESH)
    for other in range(1, sections):
        pl.semaphore_signal(
            barrier, inc=1, device_id={"section": (place + other) % sections}, device_id_type=MESH)

    def block(index):
        return pl.ds(pl.multiple_of(index * rows, rows), rows)

    def remote(src, dst, send, recv, to):
        return pltpu.make_async_remote_copy(
            src_ref=src, dst_ref=dst, send_sem=send, recv_sem=recv, device_id=to, device_id_type=MESH)

    def gate_copy(other):
        return remote(all_gates.at[block(me), :], all_gates.at[block(me), :],
                      gate_send.at[other], gate_recv.at[other], {"expert": (me + other) % experts})

    def line_copy(slot, origin, step):
        view = gathered.at[slot, block(origin * 2 + core), :]
        way = 0 if step > 0 else 1
        return remote(view, view, line_send.at[slot, way, origin], line_recv.at[slot, origin],
                      {"expert": (chip + step) * 2 + core})

    def share_copy(slot, origin, whose):
        view = gathered.at[slot, block(origin * 2 + whose), :]
        return remote(view, view, share_send.at[slot, origin], share_recv.at[slot, origin],
                      {"expert": pair})

    def pair_copy(slot, target):
        return remote(partial.at[slot, block(target * 2 + 1 - core), :], from_pair.at[slot, block(target), :],
                      pair_send.at[slot, target], pair_recv.at[slot, target], {"expert": pair})

    def chain_copy(slot, target, step):
        way = 0 if step > 0 else 1
        return remote(partial.at[slot, block(target * 2 + core), :], chain.at[slot, way, block(target), :],
                      chain_send.at[slot, target], chain_recv.at[slot, way, target],
                      {"expert": (chip + step) * 2 + core})

    def hop_copy(tick, slot, landing):
        return remote(result.at[slot], layer_in.at[tick + 1, landing],
                      hop_send.at[slot], hop_recv.at[tick, landing],
                      {"section": (place + 1) % sections})

    def done_copy(tick, target):
        return remote(result.at[1, :, target * columns:(target + 1) * columns], finished_ref.at[tick],
                      done_send.at[target], done_recv.at[tick], {"section": target})

    def done_keep(tick):
        return pltpu.make_async_copy(
            result.at[1, :, last * columns:width], finished_ref.at[tick], done_local)

    chunk = 16

    def norm(tick, slot):
        @pl.loop(0, rows // chunk)
        def _(i):
            at = pl.ds(pl.multiple_of(i * chunk, chunk), chunk)
            wide = layer_in[tick, slot, at, :].astype(jnp.float32)
            scale = lax.rsqrt(jnp.mean(wide * wide, axis=-1, keepdims=True) + EPS)
            into = pl.ds(pl.multiple_of(me * rows + i * chunk, chunk), chunk)
            gathered[slot, into, :] = (wide * scale * gain_ref[slot][None, :]).astype(jnp.bfloat16)

    def gather_begin(tick, slot):
        @pl.when(tick > 0)
        def _():
            if slot == 0:
                @pl.when(place == 0)
                def _():
                    layer_in[tick, 0] = jnp.zeros((rows, width), jnp.bfloat16)

                @pl.when(place != 0)
                def _():
                    hop_copy(tick - 1, slot, slot).wait_recv()
            else:
                hop_copy(tick - 1, slot, slot).wait_recv()
        norm(tick, slot)

        @pl.when(chip < chips - 1)
        def _():
            line_copy(slot, chip, 1).start()

        @pl.when(chip > 0)
        def _():
            line_copy(slot, chip, -1).start()
        share_copy(slot, chip, core).start()

    def gather_step(slot, k):
        for step in (1, -1):
            origin = chip - step * k
            inside = origin >= 0 if step > 0 else origin <= chips - 1
            more = chip < chips - 1 if step > 0 else chip > 0

            @pl.when(inside)
            def _():
                line_copy(slot, origin, step).wait_recv()

                @pl.when(more)
                def _():
                    line_copy(slot, origin, step).start()
                share_copy(slot, origin, core).start()

    def gather_end(slot):
        for origin in range(chips):
            share_copy(slot, origin, 1 - core).wait_recv()

    def gather_drain(slot):
        for origin in range(chips):
            share_copy(slot, origin, core).wait_send()

            @pl.when((origin <= chip) & (chip < chips - 1))
            def _():
                line_copy(slot, origin, 1).wait_send()

            @pl.when((origin >= chip) & (chip > 0))
            def _():
                line_copy(slot, origin, -1).wait_send()

    def scatter_drain(slot):
        for target in range(chips):
            pair_copy(slot, target).wait_send()

            @pl.when(target != chip)
            def _():
                chain_copy(slot, target, 1).wait_send()

    def compute(tick, slot):
        @pl.when(tick > 0)
        def _():
            scatter_drain(slot)
        total = experts * rows
        lane = lax.broadcasted_iota(jnp.int32, (rows, LANES), 1)
        here = (lane // 2) == (tick * 2 + slot)

        @pl.loop(0, experts)
        def _(j):
            chosen = jnp.where(here & (ids_ref[block(j), :] == me), all_gates[block(j), :], 0.0)
            row_gate[block(j), :] = jnp.broadcast_to(
                jnp.sum(chosen, axis=1, keepdims=True), (rows, tile))

        @pl.loop(0, hidden // tile)
        def _(n):
            at = pl.ds(pl.multiple_of(n * tile, tile), tile)
            lifted = jnp.dot(gathered[slot], up[slot, :, at], preferred_element_type=jnp.float32)
            act[:, at] = (lifted / (1.0 + jnp.exp(-lifted))).astype(jnp.bfloat16)

        @pl.loop(0, width // tile)
        def _(n):
            at = pl.ds(pl.multiple_of(n * tile, tile), tile)
            lowered = jnp.dot(act[...], down[slot, :, at], preferred_element_type=jnp.float32)
            partial[slot, :, at] = (lowered * row_gate[...]).astype(jnp.bfloat16)
        gather_drain(slot)
        for target in range(chips):
            pair_copy(slot, target).start()

    def add_to(slot, target, ways):
        mine = target * 2 + core

        @pl.loop(0, rows // chunk)
        def _(i):
            own = pl.ds(pl.multiple_of(mine * rows + i * chunk, chunk), chunk)
            there = pl.ds(pl.multiple_of(target * rows + i * chunk, chunk), chunk)
            total = partial[slot, own, :].astype(jnp.float32) + from_pair[slot, there, :].astype(jnp.float32)
            for way in ways:
                total += chain[slot, way, there, :].astype(jnp.float32)
            partial[slot, own, :] = total.astype(jnp.bfloat16)

    def scatter_send(slot, target, step, first):
        pair_copy(slot, target).wait_recv()
        if not first:
            chain_copy(slot, target, step).wait_recv()
        add_to(slot, target, () if first else ((0,) if step > 0 else (1,)))
        chain_copy(slot, target, step).start()

    def scatter_begin(slot):
        @pl.when(chip == 0)
        def _():
            for target in range(chips - 1, 0, -1):
                scatter_send(slot, target, 1, True)

        @pl.when(chip == chips - 1)
        def _():
            for target in range(chips - 1):
                scatter_send(slot, target, -1, True)

    def scatter_step(slot, k):
        @pl.when((chips - k > chip) & (chip > 0))
        def _():
            scatter_send(slot, chips - k, 1, False)

        @pl.when((k - 1 < chip) & (chip < chips - 1))
        def _():
            scatter_send(slot, k - 1, -1, False)

    def scatter_end(tick, slot):
        pair_copy(slot, chip).wait_recv()

        @pl.when(chip > 0)
        def _():
            chain_copy(slot, chip, 1).wait_recv()

        @pl.when(chip < chips - 1)
        def _():
            chain_copy(slot, chip, -1).wait_recv()

        @pl.when(chip == 0)
        def _():
            add_to(slot, chip, (1,))

        @pl.when(chip == chips - 1)
        def _():
            add_to(slot, chip, (0,))

        @pl.when((chip > 0) & (chip < chips - 1))
        def _():
            add_to(slot, chip, (0, 1))

        @pl.when(tick > 0)
        def _():
            hop_drain(slot)

        @pl.loop(0, rows // chunk)
        def _(i):
            own = pl.ds(pl.multiple_of(me * rows + i * chunk, chunk), chunk)
            at = pl.ds(pl.multiple_of(i * chunk, chunk), chunk)
            total = partial[slot, own, :].astype(jnp.float32) + layer_in[tick, slot, at, :].astype(jnp.float32)
            result[slot, at, :] = total.astype(jnp.bfloat16)

        @pl.when(place < last)
        def _():
            hop_copy(tick, slot, slot).start()

        @pl.when(place == last)
        def _():
            if slot == 0:
                hop_copy(tick, 0, 1).start()
            else:
                for target in range(last):
                    done_copy(tick, target).start()
                done_keep(tick).start()

    def hop_drain(slot):
        if slot == 0:
            hop_copy(0, 0, 0).wait_send()
        else:
            @pl.when(place < last)
            def _():
                hop_copy(0, 1, 1).wait_send()

            @pl.when(place == last)
            def _():
                for target in range(last):
                    done_copy(0, target).wait_send()
                done_keep(0).wait()

    layer_in[0] = state_ref[...]
    all_gates[block(me), :] = gates_ref[...]
    pl.semaphore_wait(barrier, experts - 1 + sections - 1)
    def half(tick, slot, other_tick, other):
        gather_begin(tick, slot)
        scatter_begin(other)
        for k in range(1, chips):
            gather_step(slot, k)
            scatter_step(other, k)
        scatter_end(other_tick, other)
        gather_end(slot)
        compute(tick, slot)

    gather_begin(0, 0)
    for other in range(1, experts):
        gate_copy(other).start()
    for k in range(1, chips):
        gather_step(0, k)
    gather_end(0)
    for load in loads:
        load.wait()
    for other in range(1, experts):
        gate_copy(other).wait_recv()
    compute(0, 0)

    half(0, 1, 0, 0)

    @pl.loop(1, tick_count)
    def _(tick):
        half(tick, 0, tick - 1, 1)
        half(tick, 1, tick, 0)

    scatter_begin(1)
    for k in range(1, chips):
        scatter_step(1, k)
    scatter_end(tick_count - 1, 1)

    for slot in range(2):
        scatter_drain(slot)
        hop_drain(slot)
    for other in range(1, experts):
        gate_copy(other).wait_send()

    @pl.when(place == 0)
    def _():
        layer_in[tick_count, 0] = jnp.zeros((rows, width), jnp.bfloat16)

    @pl.when(place != 0)
    def _():
        hop_copy(tick_count - 1, 0, 0).wait_recv()
    hop_copy(tick_count - 1, 1, 1).wait_recv()

    @pl.when(place != last)
    def _():
        for tick in range(tick_count):
            done_copy(tick, 0).wait_recv()
    final_ref[...] = layer_in[tick_count]


def tile_of(width, hidden):
    for tile in (256, 128):
        if width % tile == 0 and hidden % tile == 0:
            return tile
    return 0


def relay_bytes(ticks, experts, rows, width, hidden):
    weights = 2 * 2 * width * hidden * 2
    per_block = rows * width * 2
    blocks = 2 * (ticks + 1) + 2 * experts * 2 + experts + 2 * experts + 2 + 4
    return weights + blocks * per_block + experts * rows * (hidden * 2 + 2 * LANES * 4 + 2 * LANES * 4)


def on_device_relay(tick_count, experts, sections, tile, state, norm_gain, up_weight, down_weight, expert_ids, gate_values):
    rows, width = state.shape[2], state.shape[3]
    hidden = up_weight.shape[4]
    chips = experts // 2
    routes = jnp.transpose(expert_ids[:, :, 0], (2, 0, 1, 3)).reshape(experts * rows, tick_count * 4)
    gates = jnp.transpose(gate_values[:, :, 0], (1 + 1, 0, 1, 3)).reshape(rows, tick_count * 4)
    routes = jnp.pad(routes, ((0, 0), (0, LANES - tick_count * 4)))
    gates = jnp.pad(gates, ((0, 0), (0, LANES - tick_count * 4)))
    vmem = pl.BlockSpec(memory_space=pltpu.VMEM)
    hbm = pl.BlockSpec(memory_space=pl.ANY)
    bf16 = jnp.bfloat16
    dma = pltpu.SemaphoreType.DMA
    final, finished = pl.pallas_call(
        functools.partial(relay_kernel, tick_count, chips, sections, rows, tile),
        out_shape=(
            jax.ShapeDtypeStruct((2, rows, width), bf16),
            jax.ShapeDtypeStruct((tick_count, rows, width // sections), bf16),
        ),
        in_specs=[vmem, vmem, hbm, hbm, vmem, vmem],
        out_specs=(vmem, vmem),
        scratch_shapes=[
            pltpu.VMEM((2, width, hidden), bf16),
            pltpu.VMEM((2, hidden, width), bf16),
            pltpu.VMEM((tick_count + 1, 2, rows, width), bf16),
            pltpu.VMEM((2, experts * rows, width), bf16),
            pltpu.VMEM((2, experts * rows, width), bf16),
            pltpu.VMEM((2, chips * rows, width), bf16),
            pltpu.VMEM((2, 2, chips * rows, width), bf16),
            pltpu.VMEM((2, rows, width), bf16),
            pltpu.VMEM((experts * rows, hidden), bf16),
            pltpu.VMEM((experts * rows, tile), jnp.float32),
            pltpu.VMEM((experts * rows, LANES), jnp.float32),
            dma((4,)), dma((experts,)), dma((experts,)),
            dma((2, 2, chips)), dma((2, chips)), dma((2, chips)), dma((2, chips)),
            dma((2, chips)), dma((2, chips)), dma((2, chips)), dma((2, 2, chips)),
            dma((2,)), dma((tick_count, 2)), dma((sections,)), dma((tick_count,)), dma(()),
        ],
        compiler_params=pltpu.CompilerParams(
            collective_id=0, has_side_effects=True, vmem_limit_bytes=VMEM_LIMIT),
        cost_estimate=pl.CostEstimate(
            flops=tick_count * 2 * experts * rows * width * hidden * 4,
            bytes_accessed=8 * width * hidden, transcendentals=0),
    )(state[:, 0], norm_gain[:, 0], up_weight[:, 0, 0], down_weight[:, 0, 0], routes, gates)
    return final[:, None], finished


def from_behind(block, axis, distance):
    devices = range(lax.axis_size(axis))
    route = [((i - distance) % len(devices), i) for i in devices]
    return lax.ppermute(block, axis, route)


def spread(value, axis, root):
    mine = lax.axis_index(axis) == root
    return lax.psum(jnp.where(mine, value, jnp.zeros_like(value)), axis)


def rms_norm(layer_in, norm_gain):
    widened = layer_in.astype(jnp.float32)
    scaled = lax.rsqrt(jnp.mean(widened * widened, axis=-1, keepdims=True) + 1e-06)
    return (widened * scaled * norm_gain).astype(jnp.bfloat16)


def expert_mlp(in_rows, up_weight, down_weight):
    projected = jnp.einsum("srd,sdf->srf", in_rows, up_weight, preferred_element_type=jnp.float32)
    activated = jax.nn.silu(projected).astype(jnp.bfloat16)
    return jnp.einsum(
        "srf,sfd->srd", activated, down_weight, preferred_element_type=jnp.float32
    ).astype(jnp.bfloat16)


def source_bound(tok_rows, expert_count):
    return max(2, 4 * tok_rows // expert_count)


def through_exchange(layer_in, normed, up_weight, down_weight, routes, gates, expert_count, owner):
    slot_count, tok_rows, model_width = layer_in.shape
    per_source = source_bound(tok_rows, expert_count)
    own_routes = lax.dynamic_slice_in_dim(routes, owner * tok_rows, tok_rows, 1)
    matches = (own_routes[..., None] == jnp.arange(expert_count, dtype=jnp.int32)).astype(jnp.int32)
    flattened = matches.reshape(slot_count, tok_rows * 2, expert_count)
    picks = jnp.arange(tok_rows * 2)
    before = (picks[:, None] > picks[None, :]).astype(jnp.bfloat16)
    earlier = jnp.einsum(
        "ab,sbe->sae", before, flattened.astype(jnp.bfloat16), preferred_element_type=jnp.float32
    )
    earlier = earlier.astype(jnp.int32).reshape(slot_count, tok_rows, 2, expert_count)
    position = jnp.sum(earlier * matches, axis=3)
    slot_match = (position[..., None, None] == jnp.arange(per_source, dtype=jnp.int32)).astype(
        jnp.int32
    )
    chosen = matches[..., None] * slot_match
    dispatch = jnp.sum(chosen, axis=2).astype(jnp.bfloat16)
    weights = jnp.sum(chosen.astype(jnp.float32) * gates[..., None, None], axis=2)
    outgoing = jnp.einsum(
        "stjp,std->sjpd", dispatch, normed, preferred_element_type=jnp.float32
    ).astype(jnp.bfloat16)
    in_rows = lax.all_to_all(outgoing, "expert", split_axis=1, concat_axis=1, tiled=True)
    shaped = in_rows.reshape(slot_count, -1, model_width)
    outputs = expert_mlp(shaped, up_weight, down_weight).reshape(in_rows.shape)
    returned = lax.all_to_all(outputs, "expert", split_axis=1, concat_axis=1, tiled=True)
    combined = jnp.einsum(
        "stjp,sjpd->std", weights, returned.astype(jnp.float32), precision=lax.Precision.HIGHEST
    )
    return (layer_in.astype(jnp.float32) + combined).astype(jnp.bfloat16)


def advance(layer_in, norm_gain, up_weight, down_weight, routes, gates, expert_count, owner):
    normed = rms_norm(layer_in, norm_gain[:, None, :])
    return through_exchange(
        layer_in, normed, up_weight, down_weight, routes, gates, expert_count, owner
    )


def on_device(state, norm_gain, up_weight, down_weight, expert_ids, gate_values):
    expert_count = lax.axis_size("expert")
    segment_count = lax.axis_size("section")
    owner = lax.axis_index("expert")
    segment_place = lax.axis_index("section")
    gains = norm_gain[:, 0]
    up_local = up_weight[:, 0, 0]
    down_local = down_weight[:, 0, 0]
    current = state[:, 0]
    done_list = []
    for tick_index in range(expert_ids.shape[0]):
        routes = expert_ids[tick_index, :, 0]
        gates = gate_values[tick_index, :, 0]
        stepped = advance(current, gains, up_local, down_local, routes, gates, expert_count, owner)
        arrived = from_behind(stepped, "section", 1)
        at_start = segment_place == 0
        new_first = jnp.where(at_start, jnp.zeros_like(arrived[0]), arrived[0])
        new_second = jnp.where(at_start, arrived[0], arrived[1])
        done_list.append(arrived[1])
        current = jnp.stack([new_first, new_second])
    leaving = jnp.stack(done_list)
    leaving = spread(leaving, "section", 0)
    columns = leaving.shape[2] // segment_count
    finished = lax.dynamic_slice_in_dim(leaving, segment_place * columns, columns, 2)
    return (current[:, None], finished)


def solution(mesh):
    experts, sections = mesh.shape["expert"], mesh.shape["section"]

    def whole(state, norm_gain, up_weight, down_weight, expert_ids, gate_values):
        ticks = expert_ids.shape[0]
        rows, width, hidden = state.shape[2] // experts, state.shape[3], up_weight.shape[4]
        tile = tile_of(width, hidden)
        fits = (
            experts % 2 == 0 and experts >= 4 and sections >= 2 and rows % 16 == 0 and tile
            and width % (sections * LANES) == 0 and ticks * 4 <= LANES
            and relay_bytes(ticks, experts, rows, width, hidden) <= VMEM_BUDGET
        )
        body = on_device
        if fits:
            body = functools.partial(on_device_relay, ticks, experts, sections, tile)
        return jax.shard_map(
            body,
            mesh=mesh,
            in_specs=(
                P(None, "section", "expert", None),
                P(None, "section", None),
                P(None, "section", "expert", None, None),
                P(None, "section", "expert", None, None),
                P(None, None, "section", None, None),
                P(None, None, "section", "expert", None),
            ),
            out_specs=(P(None, "section", "expert", None), P(None, "expert", "section")),
            check_vma=False,
        )(state, norm_gain, up_weight, down_weight, expert_ids, gate_values)

    return whole
```

```python
import functools

import jax
import jax.numpy as jnp
from jax import lax
from jax.experimental import pallas as pl
from jax.experimental.pallas import tpu as pltpu
from jax.sharding import PartitionSpec as P

EPS = 1e-06
LANES = 128
VMEM_LIMIT = 60 * 1024 * 1024
VMEM_BUDGET = 44 * 1024 * 1024
MESH = pl.DeviceIdType.MESH


def relay_kernel(
    tick_count, chips, sections, rows, tile,
    state_ref, gain_ref, up_hbm, down_hbm, ids_ref, gates_ref,
    final_ref, finished_ref,
    up, down, layer_in, gathered, partial, from_pair, chain, result, act, row_gate, all_gates,
    load_sem, gate_send, gate_recv,
    line_send, line_recv, share_send, share_recv,
    pair_send, pair_recv, chain_send, chain_recv,
    hop_send, hop_recv, done_send, done_recv, done_local,
):
    width = layer_in.shape[3]
    hidden = up.shape[2]
    experts = 2 * chips
    me = lax.axis_index("expert")
    place = lax.axis_index("section")
    chip, core = me // 2, me % 2
    pair = chip * 2 + 1 - core
    last = sections - 1
    columns = width // sections

    loads = [pltpu.make_async_copy(up_hbm.at[c], up.at[c], load_sem.at[c]) for c in range(2)]
    loads += [pltpu.make_async_copy(down_hbm.at[c], down.at[c], load_sem.at[2 + c]) for c in range(2)]
    for load in loads:
        load.start()

    barrier = pltpu.get_barrier_semaphore()
    for other in range(1, experts):
        pl.semaphore_signal(
            barrier, inc=1, device_id={"expert": (me + other) % experts}, device_id_type=MESH)
    for other in range(1, sections):
        pl.semaphore_signal(
            barrier, inc=1, device_id={"section": (place + other) % sections}, device_id_type=MESH)

    chunk = 16
    halves = 2 if rows % (2 * chunk) == 0 else 1
    sub = rows // halves

    def part(index, h):
        return pl.ds(pl.multiple_of(index * rows + h * sub, sub), sub)

    def block(index):
        return pl.ds(pl.multiple_of(index * rows, rows), rows)

    def remote(src, dst, send, recv, to):
        return pltpu.make_async_remote_copy(
            src_ref=src, dst_ref=dst, send_sem=send, recv_sem=recv, device_id=to, device_id_type=MESH)

    def gate_copy(other):
        return remote(all_gates.at[block(me), :], all_gates.at[block(me), :],
                      gate_send.at[other], gate_recv.at[other], {"expert": (me + other) % experts})

    def line_copy(slot, origin, step, h):
        view = gathered.at[slot, part(origin * 2 + core, h), :]
        way = 0 if step > 0 else 1
        return remote(view, view, line_send.at[slot, way, origin, h], line_recv.at[slot, origin, h],
                      {"expert": (chip + step) * 2 + core})

    def share_copy(slot, origin, whose):
        view = gathered.at[slot, block(origin * 2 + whose), :]
        return remote(view, view, share_send.at[slot, origin], share_recv.at[slot, origin],
                      {"expert": pair})

    def pair_copy(slot, target):
        return remote(partial.at[slot, block(target * 2 + 1 - core), :], from_pair.at[slot, block(target), :],
                      pair_send.at[slot, target], pair_recv.at[slot, target], {"expert": pair})

    def chain_copy(slot, target, step, h):
        way = 0 if step > 0 else 1
        return remote(partial.at[slot, part(target * 2 + core, h), :], chain.at[slot, way, part(target, h), :],
                      chain_send.at[slot, target, h], chain_recv.at[slot, way, target, h],
                      {"expert": (chip + step) * 2 + core})

    def hop_copy(tick, slot, landing, h):
        return remote(result.at[slot, part(0, h), :], layer_in.at[tick + 1, landing, part(0, h), :],
                      hop_send.at[slot, h], hop_recv.at[tick, landing, h],
                      {"section": (place + 1) % sections})

    def done_copy(tick, target):
        return remote(result.at[1, :, target * columns:(target + 1) * columns], finished_ref.at[tick],
                      done_send.at[target], done_recv.at[tick], {"section": target})

    def done_keep(tick):
        return pltpu.make_async_copy(
            result.at[1, :, last * columns:width], finished_ref.at[tick], done_local)

    def norm(tick, slot, h):
        @pl.loop(0, sub // chunk)
        def _(i):
            at = pl.ds(pl.multiple_of(h * sub + i * chunk, chunk), chunk)
            wide = layer_in[tick, slot, at, :].astype(jnp.float32)
            scale = lax.rsqrt(jnp.mean(wide * wide, axis=-1, keepdims=True) + EPS)
            into = pl.ds(pl.multiple_of(me * rows + h * sub + i * chunk, chunk), chunk)
            gathered[slot, into, :] = (wide * scale * gain_ref[slot][None, :]).astype(jnp.bfloat16)

    def hop_arrive(tick, slot, h):
        if slot == 0:
            @pl.when(place == 0)
            def _():
                layer_in[tick, 0, h * sub:(h + 1) * sub, :] = jnp.zeros((sub, width), jnp.bfloat16)

            @pl.when(place != 0)
            def _():
                hop_copy(tick - 1, slot, slot, h).wait_recv()
        else:
            hop_copy(tick - 1, slot, slot, h).wait_recv()

    def gather_begin(tick, slot):
        for h in range(halves):
            @pl.when(tick > 0)
            def _():
                hop_arrive(tick, slot, h)
            norm(tick, slot, h)

            @pl.when(chip < chips - 1)
            def _():
                line_copy(slot, chip, 1, h).start()

            @pl.when(chip > 0)
            def _():
                line_copy(slot, chip, -1, h).start()
        share_copy(slot, chip, core).start()

    def gather_step(slot, k, h):
        for step in (1, -1):
            origin = chip - step * k
            inside = origin >= 0 if step > 0 else origin <= chips - 1
            more = chip < chips - 1 if step > 0 else chip > 0

            @pl.when(inside)
            def _():
                line_copy(slot, origin, step, h).wait_recv()

                @pl.when(more)
                def _():
                    line_copy(slot, origin, step, h).start()
                if h == halves - 1:
                    share_copy(slot, origin, core).start()

    def gather_end(slot):
        for origin in range(chips):
            share_copy(slot, origin, 1 - core).wait_recv()

    def gather_drain(slot):
        for origin in range(chips):
            share_copy(slot, origin, core).wait_send()
            for h in range(halves):
                @pl.when((origin <= chip) & (chip < chips - 1))
                def _():
                    line_copy(slot, origin, 1, h).wait_send()

                @pl.when((origin >= chip) & (chip > 0))
                def _():
                    line_copy(slot, origin, -1, h).wait_send()

    def scatter_drain(slot):
        for target in range(chips):
            pair_copy(slot, target).wait_send()

            @pl.when(target != chip)
            def _():
                for h in range(halves):
                    chain_copy(slot, target, 1, h).wait_send()

    def compute_up(tick, slot):
        lane = lax.broadcasted_iota(jnp.int32, (rows, LANES), 1)
        here = (lane // 2) == (tick * 2 + slot)

        @pl.loop(0, experts)
        def _(j):
            chosen = jnp.where(here & (ids_ref[block(j), :] == me), all_gates[block(j), :], 0.0)
            row_gate[block(j), :] = jnp.broadcast_to(
                jnp.sum(chosen, axis=1, keepdims=True), (rows, tile))

        @pl.loop(0, hidden // tile)
        def _(n):
            at = pl.ds(pl.multiple_of(n * tile, tile), tile)
            lifted = jnp.dot(gathered[slot], up[slot, :, at], preferred_element_type=jnp.float32)
            act[:, at] = (lifted / (1.0 + jnp.exp(-lifted))).astype(jnp.bfloat16)
        gather_drain(slot)

    def compute_down(tick, slot):
        @pl.when(tick > 0)
        def _():
            scatter_drain(slot)

        @pl.loop(0, width // tile)
        def _(n):
            at = pl.ds(pl.multiple_of(n * tile, tile), tile)
            lowered = jnp.dot(act[...], down[slot, :, at], preferred_element_type=jnp.float32)
            partial[slot, :, at] = (lowered * row_gate[...]).astype(jnp.bfloat16)
        for target in range(chips):
            pair_copy(slot, target).start()

    def summed(slot, target, ways, start):
        own = pl.ds(pl.multiple_of(target * 2 * rows + core * rows + start, chunk), chunk)
        there = pl.ds(pl.multiple_of(target * rows + start, chunk), chunk)
        total = partial[slot, own, :].astype(jnp.float32) + from_pair[slot, there, :].astype(jnp.float32)
        for way in ways:
            total += chain[slot, way, there, :].astype(jnp.float32)
        return own, total

    def add_to(slot, target, ways, h):
        @pl.loop(0, sub // chunk)
        def _(i):
            own, total = summed(slot, target, ways, h * sub + i * chunk)
            partial[slot, own, :] = total.astype(jnp.bfloat16)

    def finish(tick, slot, ways, h):
        @pl.loop(0, sub // chunk)
        def _(i):
            _, total = summed(slot, chip, ways, h * sub + i * chunk)
            at = pl.ds(pl.multiple_of(h * sub + i * chunk, chunk), chunk)
            result[slot, at, :] = (total + layer_in[tick, slot, at, :].astype(jnp.float32)).astype(jnp.bfloat16)

    def scatter_step(slot, turn, h):
        for step in (1, -1):
            target = chip + step * (chips - turn + 1)
            inside = (target <= chips - 1) if step > 0 else (target >= 0)
            first = chip == 0 if step > 0 else chip == chips - 1

            @pl.when(inside)
            def _():
                if h == 0:
                    pair_copy(slot, target).wait_recv()

                @pl.when(first)
                def _():
                    add_to(slot, target, (), h)

                @pl.when(jnp.logical_not(first))
                def _():
                    chain_copy(slot, target, step, h).wait_recv()
                    add_to(slot, target, (0,) if step > 0 else (1,), h)
                chain_copy(slot, target, step, h).start()

    def scatter_end(tick, slot):
        pair_copy(slot, chip).wait_recv()

        @pl.when(tick > 0)
        def _():
            hop_drain(slot)
        for h in range(halves):
            @pl.when(chip > 0)
            def _():
                chain_copy(slot, chip, 1, h).wait_recv()

            @pl.when(chip < chips - 1)
            def _():
                chain_copy(slot, chip, -1, h).wait_recv()

            @pl.when(chip == 0)
            def _():
                finish(tick, slot, (1,), h)

            @pl.when(chip == chips - 1)
            def _():
                finish(tick, slot, (0,), h)

            @pl.when((chip > 0) & (chip < chips - 1))
            def _():
                finish(tick, slot, (0, 1), h)

            @pl.when(place < last)
            def _():
                hop_copy(tick, slot, slot, h).start()
            if slot == 0:
                @pl.when(place == last)
                def _():
                    hop_copy(tick, 0, 1, h).start()
        if slot == 1:
            @pl.when(place == last)
            def _():
                for target in range(last):
                    done_copy(tick, target).start()
                done_keep(tick).start()

    def hop_drain(slot):
        if slot == 0:
            for h in range(halves):
                hop_copy(0, 0, 0, h).wait_send()
        else:
            @pl.when(place < last)
            def _():
                for h in range(halves):
                    hop_copy(0, 1, 1, h).wait_send()

            @pl.when(place == last)
            def _():
                for target in range(last):
                    done_copy(0, target).wait_send()
                done_keep(0).wait()

    def half(tick, slot, other_tick, other):
        gather_begin(tick, slot)
        for turn in range(1, chips + 1):
            for h in range(halves):
                if turn > 1:
                    gather_step(slot, turn - 1, h)
                    scatter_step(other, turn, h)
        gather_end(slot)
        compute_up(tick, slot)
        scatter_end(other_tick, other)
        compute_down(tick, slot)

    layer_in[0] = state_ref[...]
    all_gates[block(me), :] = gates_ref[...]
    pl.semaphore_wait(barrier, experts - 1 + sections - 1)

    gather_begin(0, 0)
    for other in range(1, experts):
        gate_copy(other).start()
    for k in range(1, chips):
        for h in range(halves):
            gather_step(0, k, h)
    gather_end(0)
    for load in loads:
        load.wait()
    for other in range(1, experts):
        gate_copy(other).wait_recv()
    compute_up(0, 0)
    compute_down(0, 0)

    half(0, 1, 0, 0)

    @pl.loop(1, tick_count)
    def _(tick):
        half(tick, 0, tick - 1, 1)
        half(tick, 1, tick, 0)

    for turn in range(2, chips + 1):
        for h in range(halves):
            scatter_step(1, turn, h)
    scatter_end(tick_count - 1, 1)

    for slot in range(2):
        scatter_drain(slot)
        hop_drain(slot)
    for other in range(1, experts):
        gate_copy(other).wait_send()
    for h in range(halves):
        hop_arrive(tick_count, 0, h)
        hop_arrive(tick_count, 1, h)

    @pl.when(place != last)
    def _():
        for tick in range(tick_count):
            done_copy(tick, 0).wait_recv()
    final_ref[...] = layer_in[tick_count]


def tile_of(width, hidden):
    for tile in (256, 128):
        if width % tile == 0 and hidden % tile == 0:
            return tile
    return 0


def relay_bytes(ticks, experts, rows, width, hidden):
    weights = 2 * 2 * width * hidden * 2
    per_block = rows * width * 2
    blocks = 2 * (ticks + 1) + 2 * experts * 2 + experts + 2 * experts + 2 + 4
    return weights + blocks * per_block + experts * rows * (hidden * 2 + 2 * LANES * 4 + 2 * LANES * 4)


def on_device_relay(tick_count, experts, sections, tile, state, norm_gain, up_weight, down_weight, expert_ids, gate_values):
    rows, width = state.shape[2], state.shape[3]
    hidden = up_weight.shape[4]
    chips = experts // 2
    routes = jnp.transpose(expert_ids[:, :, 0], (2, 0, 1, 3)).reshape(experts * rows, tick_count * 4)
    gates = jnp.transpose(gate_values[:, :, 0], (1 + 1, 0, 1, 3)).reshape(rows, tick_count * 4)
    routes = jnp.pad(routes, ((0, 0), (0, LANES - tick_count * 4)))
    gates = jnp.pad(gates, ((0, 0), (0, LANES - tick_count * 4)))
    vmem = pl.BlockSpec(memory_space=pltpu.VMEM)
    hbm = pl.BlockSpec(memory_space=pl.ANY)
    bf16 = jnp.bfloat16
    dma = pltpu.SemaphoreType.DMA
    final, finished = pl.pallas_call(
        functools.partial(relay_kernel, tick_count, chips, sections, rows, tile),
        out_shape=(
            jax.ShapeDtypeStruct((2, rows, width), bf16),
            jax.ShapeDtypeStruct((tick_count, rows, width // sections), bf16),
        ),
        in_specs=[vmem, vmem, hbm, hbm, vmem, vmem],
        out_specs=(vmem, vmem),
        scratch_shapes=[
            pltpu.VMEM((2, width, hidden), bf16),
            pltpu.VMEM((2, hidden, width), bf16),
            pltpu.VMEM((tick_count + 1, 2, rows, width), bf16),
            pltpu.VMEM((2, experts * rows, width), bf16),
            pltpu.VMEM((2, experts * rows, width), bf16),
            pltpu.VMEM((2, chips * rows, width), bf16),
            pltpu.VMEM((2, 2, chips * rows, width), bf16),
            pltpu.VMEM((2, rows, width), bf16),
            pltpu.VMEM((experts * rows, hidden), bf16),
            pltpu.VMEM((experts * rows, tile), jnp.float32),
            pltpu.VMEM((experts * rows, LANES), jnp.float32),
            dma((4,)), dma((experts,)), dma((experts,)),
            dma((2, 2, chips, 2)), dma((2, chips, 2)), dma((2, chips)), dma((2, chips)),
            dma((2, chips)), dma((2, chips)), dma((2, chips, 2)), dma((2, 2, chips, 2)),
            dma((2, 2)), dma((tick_count, 2, 2)), dma((sections,)), dma((tick_count,)), dma(()),
        ],
        compiler_params=pltpu.CompilerParams(
            collective_id=0, has_side_effects=True, vmem_limit_bytes=VMEM_LIMIT),
        cost_estimate=pl.CostEstimate(
            flops=tick_count * 2 * experts * rows * width * hidden * 4,
            bytes_accessed=8 * width * hidden, transcendentals=0),
    )(state[:, 0], norm_gain[:, 0], up_weight[:, 0, 0], down_weight[:, 0, 0], routes, gates)
    return final[:, None], finished


def from_behind(block, axis, distance):
    devices = range(lax.axis_size(axis))
    route = [((i - distance) % len(devices), i) for i in devices]
    return lax.ppermute(block, axis, route)


def spread(value, axis, root):
    mine = lax.axis_index(axis) == root
    return lax.psum(jnp.where(mine, value, jnp.zeros_like(value)), axis)


def rms_norm(layer_in, norm_gain):
    widened = layer_in.astype(jnp.float32)
    scaled = lax.rsqrt(jnp.mean(widened * widened, axis=-1, keepdims=True) + 1e-06)
    return (widened * scaled * norm_gain).astype(jnp.bfloat16)


def expert_mlp(in_rows, up_weight, down_weight):
    projected = jnp.einsum("srd,sdf->srf", in_rows, up_weight, preferred_element_type=jnp.float32)
    activated = jax.nn.silu(projected).astype(jnp.bfloat16)
    return jnp.einsum(
        "srf,sfd->srd", activated, down_weight, preferred_element_type=jnp.float32
    ).astype(jnp.bfloat16)


def source_bound(tok_rows, expert_count):
    return max(2, 4 * tok_rows // expert_count)


def through_exchange(layer_in, normed, up_weight, down_weight, routes, gates, expert_count, owner):
    slot_count, tok_rows, model_width = layer_in.shape
    per_source = source_bound(tok_rows, expert_count)
    own_routes = lax.dynamic_slice_in_dim(routes, owner * tok_rows, tok_rows, 1)
    matches = (own_routes[..., None] == jnp.arange(expert_count, dtype=jnp.int32)).astype(jnp.int32)
    flattened = matches.reshape(slot_count, tok_rows * 2, expert_count)
    picks = jnp.arange(tok_rows * 2)
    before = (picks[:, None] > picks[None, :]).astype(jnp.bfloat16)
    earlier = jnp.einsum(
        "ab,sbe->sae", before, flattened.astype(jnp.bfloat16), preferred_element_type=jnp.float32
    )
    earlier = earlier.astype(jnp.int32).reshape(slot_count, tok_rows, 2, expert_count)
    position = jnp.sum(earlier * matches, axis=3)
    slot_match = (position[..., None, None] == jnp.arange(per_source, dtype=jnp.int32)).astype(
        jnp.int32
    )
    chosen = matches[..., None] * slot_match
    dispatch = jnp.sum(chosen, axis=2).astype(jnp.bfloat16)
    weights = jnp.sum(chosen.astype(jnp.float32) * gates[..., None, None], axis=2)
    outgoing = jnp.einsum(
        "stjp,std->sjpd", dispatch, normed, preferred_element_type=jnp.float32
    ).astype(jnp.bfloat16)
    in_rows = lax.all_to_all(outgoing, "expert", split_axis=1, concat_axis=1, tiled=True)
    shaped = in_rows.reshape(slot_count, -1, model_width)
    outputs = expert_mlp(shaped, up_weight, down_weight).reshape(in_rows.shape)
    returned = lax.all_to_all(outputs, "expert", split_axis=1, concat_axis=1, tiled=True)
    combined = jnp.einsum(
        "stjp,sjpd->std", weights, returned.astype(jnp.float32), precision=lax.Precision.HIGHEST
    )
    return (layer_in.astype(jnp.float32) + combined).astype(jnp.bfloat16)


def advance(layer_in, norm_gain, up_weight, down_weight, routes, gates, expert_count, owner):
    normed = rms_norm(layer_in, norm_gain[:, None, :])
    return through_exchange(
        layer_in, normed, up_weight, down_weight, routes, gates, expert_count, owner
    )


def on_device(state, norm_gain, up_weight, down_weight, expert_ids, gate_values):
    expert_count = lax.axis_size("expert")
    segment_count = lax.axis_size("section")
    owner = lax.axis_index("expert")
    segment_place = lax.axis_index("section")
    gains = norm_gain[:, 0]
    up_local = up_weight[:, 0, 0]
    down_local = down_weight[:, 0, 0]
    current = state[:, 0]
    done_list = []
    for tick_index in range(expert_ids.shape[0]):
        routes = expert_ids[tick_index, :, 0]
        gates = gate_values[tick_index, :, 0]
        stepped = advance(current, gains, up_local, down_local, routes, gates, expert_count, owner)
        arrived = from_behind(stepped, "section", 1)
        at_start = segment_place == 0
        new_first = jnp.where(at_start, jnp.zeros_like(arrived[0]), arrived[0])
        new_second = jnp.where(at_start, arrived[0], arrived[1])
        done_list.append(arrived[1])
        current = jnp.stack([new_first, new_second])
    leaving = jnp.stack(done_list)
    leaving = spread(leaving, "section", 0)
    columns = leaving.shape[2] // segment_count
    finished = lax.dynamic_slice_in_dim(leaving, segment_place * columns, columns, 2)
    return (current[:, None], finished)


def solution(mesh):
    experts, sections = mesh.shape["expert"], mesh.shape["section"]

    def whole(state, norm_gain, up_weight, down_weight, expert_ids, gate_values):
        ticks = expert_ids.shape[0]
        rows, width, hidden = state.shape[2] // experts, state.shape[3], up_weight.shape[4]
        tile = tile_of(width, hidden)
        fits = (
            experts % 2 == 0 and experts >= 4 and sections >= 2 and rows % 16 == 0 and tile
            and width % (sections * LANES) == 0 and ticks * 4 <= LANES
            and relay_bytes(ticks, experts, rows, width, hidden) <= VMEM_BUDGET
        )
        body = on_device
        if fits:
            body = functools.partial(on_device_relay, ticks, experts, sections, tile)
        return jax.shard_map(
            body,
            mesh=mesh,
            in_specs=(
                P(None, "section", "expert", None),
                P(None, "section", None),
                P(None, "section", "expert", None, None),
                P(None, "section", "expert", None, None),
                P(None, None, "section", None, None),
                P(None, None, "section", "expert", None),
            ),
            out_specs=(P(None, "section", "expert", None), P(None, "expert", "section")),
            check_vma=False,
        )(state, norm_gain, up_weight, down_weight, expert_ids, gate_values)

    return whole
```

```python
import functools

import jax
import jax.numpy as jnp
from jax import lax
from jax.experimental import pallas as pl
from jax.experimental.pallas import tpu as pltpu
from jax.sharding import PartitionSpec as P

EPS = 1e-06
LANES = 128
VMEM_LIMIT = 60 * 1024 * 1024
VMEM_BUDGET = 44 * 1024 * 1024
MESH = pl.DeviceIdType.MESH


def relay_kernel(
    tick_count, chips, sections, rows, tile,
    state_ref, gain_ref, up_hbm, down_hbm, ids_ref, gates_ref,
    final_ref, finished_ref,
    up, down, layer_in, gathered, partial, from_pair, chain, result, act, row_gate, all_gates,
    load_sem, gate_send, gate_recv,
    line_send, line_recv, share_send, share_recv,
    pair_send, pair_recv, chain_send, chain_recv,
    hop_send, hop_recv, done_send, done_recv, done_local,
):
    width = layer_in.shape[3]
    hidden = up.shape[2]
    experts = 2 * chips
    me = lax.axis_index("expert")
    place = lax.axis_index("section")
    chip, core = me // 2, me % 2
    pair = chip * 2 + 1 - core
    last = sections - 1
    columns = width // sections

    loads = [pltpu.make_async_copy(up_hbm.at[c], up.at[c], load_sem.at[c]) for c in range(2)]
    loads += [pltpu.make_async_copy(down_hbm.at[c], down.at[c], load_sem.at[2 + c]) for c in range(2)]
    for load in loads:
        load.start()

    barrier = pltpu.get_barrier_semaphore()
    for other in range(1, experts):
        pl.semaphore_signal(
            barrier, inc=1, device_id={"expert": (me + other) % experts}, device_id_type=MESH)
    for other in range(1, sections):
        pl.semaphore_signal(
            barrier, inc=1, device_id={"section": (place + other) % sections}, device_id_type=MESH)

    chunk = 16
    halves = next(h for h in (4, 2, 1) if rows % (h * chunk) == 0)
    sub = rows // halves

    def part(index, h):
        return pl.ds(pl.multiple_of(index * rows + h * sub, sub), sub)

    def block(index):
        return pl.ds(pl.multiple_of(index * rows, rows), rows)

    def remote(src, dst, send, recv, to):
        return pltpu.make_async_remote_copy(
            src_ref=src, dst_ref=dst, send_sem=send, recv_sem=recv, device_id=to, device_id_type=MESH)

    def gate_copy(other):
        return remote(all_gates.at[block(me), :], all_gates.at[block(me), :],
                      gate_send.at[other], gate_recv.at[other], {"expert": (me + other) % experts})

    def line_copy(slot, origin, step, h):
        view = gathered.at[slot, part(origin * 2 + core, h), :]
        way = 0 if step > 0 else 1
        return remote(view, view, line_send.at[slot, way, origin, h], line_recv.at[slot, origin, h],
                      {"expert": (chip + step) * 2 + core})

    def share_copy(slot, origin, whose):
        view = gathered.at[slot, block(origin * 2 + whose), :]
        return remote(view, view, share_send.at[slot, origin], share_recv.at[slot, origin],
                      {"expert": pair})

    def pair_copy(slot, target):
        return remote(partial.at[slot, block(target * 2 + 1 - core), :], from_pair.at[slot, block(target), :],
                      pair_send.at[slot, target], pair_recv.at[slot, target], {"expert": pair})

    def chain_copy(slot, target, step, h):
        way = 0 if step > 0 else 1
        return remote(partial.at[slot, part(target * 2 + core, h), :], chain.at[slot, way, part(target, h), :],
                      chain_send.at[slot, target, h], chain_recv.at[slot, way, target, h],
                      {"expert": (chip + step) * 2 + core})

    def hop_copy(tick, slot, landing, h):
        return remote(result.at[slot, part(0, h), :], layer_in.at[tick + 1, landing, part(0, h), :],
                      hop_send.at[slot, h], hop_recv.at[tick, landing, h],
                      {"section": (place + 1) % sections})

    def done_copy(tick, target):
        return remote(result.at[1, :, target * columns:(target + 1) * columns], finished_ref.at[tick],
                      done_send.at[target], done_recv.at[tick], {"section": target})

    def done_keep(tick):
        return pltpu.make_async_copy(
            result.at[1, :, last * columns:width], finished_ref.at[tick], done_local)

    def norm(tick, slot, h):
        @pl.loop(0, sub // chunk)
        def _(i):
            at = pl.ds(pl.multiple_of(h * sub + i * chunk, chunk), chunk)
            wide = layer_in[tick, slot, at, :].astype(jnp.float32)
            scale = lax.rsqrt(jnp.mean(wide * wide, axis=-1, keepdims=True) + EPS)
            into = pl.ds(pl.multiple_of(me * rows + h * sub + i * chunk, chunk), chunk)
            gathered[slot, into, :] = (wide * scale * gain_ref[slot][None, :]).astype(jnp.bfloat16)

    def hop_arrive(tick, slot, h):
        if slot == 0:
            @pl.when(place == 0)
            def _():
                layer_in[tick, 0, h * sub:(h + 1) * sub, :] = jnp.zeros((sub, width), jnp.bfloat16)

            @pl.when(place != 0)
            def _():
                hop_copy(tick - 1, slot, slot, h).wait_recv()
        else:
            hop_copy(tick - 1, slot, slot, h).wait_recv()

    def gather_begin(tick, slot):
        for h in range(halves):
            @pl.when(tick > 0)
            def _():
                hop_arrive(tick, slot, h)
            norm(tick, slot, h)

            @pl.when(chip < chips - 1)
            def _():
                line_copy(slot, chip, 1, h).start()

            @pl.when(chip > 0)
            def _():
                line_copy(slot, chip, -1, h).start()
        share_copy(slot, chip, core).start()

    def gather_step(slot, k, h):
        for step in (1, -1):
            origin = chip - step * k
            inside = origin >= 0 if step > 0 else origin <= chips - 1
            more = chip < chips - 1 if step > 0 else chip > 0

            @pl.when(inside)
            def _():
                line_copy(slot, origin, step, h).wait_recv()

                @pl.when(more)
                def _():
                    line_copy(slot, origin, step, h).start()
                if h == halves - 1:
                    share_copy(slot, origin, core).start()

    def gather_end(slot):
        for origin in range(chips):
            share_copy(slot, origin, 1 - core).wait_recv()

    def gather_drain(slot):
        for origin in range(chips):
            share_copy(slot, origin, core).wait_send()
            for h in range(halves):
                @pl.when((origin <= chip) & (chip < chips - 1))
                def _():
                    line_copy(slot, origin, 1, h).wait_send()

                @pl.when((origin >= chip) & (chip > 0))
                def _():
                    line_copy(slot, origin, -1, h).wait_send()

    def scatter_drain(slot):
        for target in range(chips):
            pair_copy(slot, target).wait_send()

            @pl.when(target != chip)
            def _():
                for h in range(halves):
                    chain_copy(slot, target, 1, h).wait_send()

    def compute_up(tick, slot):
        lane = lax.broadcasted_iota(jnp.int32, (rows, LANES), 1)
        here = (lane // 2) == (tick * 2 + slot)

        @pl.loop(0, experts)
        def _(j):
            chosen = jnp.where(here & (ids_ref[block(j), :] == me), all_gates[block(j), :], 0.0)
            row_gate[block(j), :] = jnp.broadcast_to(
                jnp.sum(chosen, axis=1, keepdims=True), (rows, tile))

        @pl.loop(0, hidden // tile)
        def _(n):
            at = pl.ds(pl.multiple_of(n * tile, tile), tile)
            lifted = jnp.dot(gathered[slot], up[slot, :, at], preferred_element_type=jnp.float32)
            act[:, at] = (lifted / (1.0 + jnp.exp(-lifted))).astype(jnp.bfloat16)
        gather_drain(slot)

    def compute_down(tick, slot):
        @pl.when(tick > 0)
        def _():
            scatter_drain(slot)

        @pl.loop(0, width // tile)
        def _(n):
            at = pl.ds(pl.multiple_of(n * tile, tile), tile)
            lowered = jnp.dot(act[...], down[slot, :, at], preferred_element_type=jnp.float32)
            partial[slot, :, at] = (lowered * row_gate[...]).astype(jnp.bfloat16)
        for target in range(chips):
            pair_copy(slot, target).start()

    def summed(slot, target, ways, start):
        own = pl.ds(pl.multiple_of(target * 2 * rows + core * rows + start, chunk), chunk)
        there = pl.ds(pl.multiple_of(target * rows + start, chunk), chunk)
        total = partial[slot, own, :].astype(jnp.float32) + from_pair[slot, there, :].astype(jnp.float32)
        for way in ways:
            total += chain[slot, way, there, :].astype(jnp.float32)
        return own, total

    def add_to(slot, target, ways, h):
        @pl.loop(0, sub // chunk)
        def _(i):
            own, total = summed(slot, target, ways, h * sub + i * chunk)
            partial[slot, own, :] = total.astype(jnp.bfloat16)

    def finish(tick, slot, ways, h):
        @pl.loop(0, sub // chunk)
        def _(i):
            _, total = summed(slot, chip, ways, h * sub + i * chunk)
            at = pl.ds(pl.multiple_of(h * sub + i * chunk, chunk), chunk)
            result[slot, at, :] = (total + layer_in[tick, slot, at, :].astype(jnp.float32)).astype(jnp.bfloat16)

    def scatter_step(slot, turn, h):
        for step in (1, -1):
            target = chip + step * (chips - turn + 1)
            inside = (target <= chips - 1) if step > 0 else (target >= 0)
            first = chip == 0 if step > 0 else chip == chips - 1

            @pl.when(inside)
            def _():
                if h == 0:
                    pair_copy(slot, target).wait_recv()

                @pl.when(first)
                def _():
                    add_to(slot, target, (), h)

                @pl.when(jnp.logical_not(first))
                def _():
                    chain_copy(slot, target, step, h).wait_recv()
                    add_to(slot, target, (0,) if step > 0 else (1,), h)
                chain_copy(slot, target, step, h).start()

    def scatter_end(tick, slot):
        pair_copy(slot, chip).wait_recv()

        @pl.when(tick > 0)
        def _():
            hop_drain(slot)
        for h in range(halves):
            @pl.when(chip > 0)
            def _():
                chain_copy(slot, chip, 1, h).wait_recv()

            @pl.when(chip < chips - 1)
            def _():
                chain_copy(slot, chip, -1, h).wait_recv()

            @pl.when(chip == 0)
            def _():
                finish(tick, slot, (1,), h)

            @pl.when(chip == chips - 1)
            def _():
                finish(tick, slot, (0,), h)

            @pl.when((chip > 0) & (chip < chips - 1))
            def _():
                finish(tick, slot, (0, 1), h)

            @pl.when(place < last)
            def _():
                hop_copy(tick, slot, slot, h).start()
            if slot == 0:
                @pl.when(place == last)
                def _():
                    hop_copy(tick, 0, 1, h).start()
        if slot == 1:
            @pl.when(place == last)
            def _():
                for target in range(last):
                    done_copy(tick, target).start()
                done_keep(tick).start()

    def hop_drain(slot):
        if slot == 0:
            for h in range(halves):
                hop_copy(0, 0, 0, h).wait_send()
        else:
            @pl.when(place < last)
            def _():
                for h in range(halves):
                    hop_copy(0, 1, 1, h).wait_send()

            @pl.when(place == last)
            def _():
                for target in range(last):
                    done_copy(0, target).wait_send()
                done_keep(0).wait()

    def half(tick, slot, other_tick, other):
        gather_begin(tick, slot)
        for turn in range(1, chips + 1):
            for h in range(halves):
                if turn > 1:
                    gather_step(slot, turn - 1, h)
                    scatter_step(other, turn, h)
        gather_end(slot)
        compute_up(tick, slot)
        scatter_end(other_tick, other)
        compute_down(tick, slot)

    layer_in[0] = state_ref[...]
    all_gates[block(me), :] = gates_ref[...]
    pl.semaphore_wait(barrier, experts - 1 + sections - 1)

    gather_begin(0, 0)
    for other in range(1, experts):
        gate_copy(other).start()
    for k in range(1, chips):
        for h in range(halves):
            gather_step(0, k, h)
    gather_end(0)
    for load in loads:
        load.wait()
    for other in range(1, experts):
        gate_copy(other).wait_recv()
    compute_up(0, 0)
    compute_down(0, 0)

    half(0, 1, 0, 0)

    @pl.loop(1, tick_count)
    def _(tick):
        half(tick, 0, tick - 1, 1)
        half(tick, 1, tick, 0)

    for turn in range(2, chips + 1):
        for h in range(halves):
            scatter_step(1, turn, h)
    scatter_end(tick_count - 1, 1)

    for slot in range(2):
        scatter_drain(slot)
        hop_drain(slot)
    for other in range(1, experts):
        gate_copy(other).wait_send()
    for h in range(halves):
        hop_arrive(tick_count, 0, h)
        hop_arrive(tick_count, 1, h)

    @pl.when(place != last)
    def _():
        for tick in range(tick_count):
            done_copy(tick, 0).wait_recv()
    final_ref[...] = layer_in[tick_count]


def tile_of(width, hidden):
    for tile in (256, 128):
        if width % tile == 0 and hidden % tile == 0:
            return tile
    return 0


def relay_bytes(ticks, experts, rows, width, hidden):
    weights = 2 * 2 * width * hidden * 2
    per_block = rows * width * 2
    blocks = 2 * (ticks + 1) + 2 * experts * 2 + experts + 2 * experts + 2 + 4
    return weights + blocks * per_block + experts * rows * (hidden * 2 + 2 * LANES * 4 + 2 * LANES * 4)


def on_device_relay(tick_count, experts, sections, tile, state, norm_gain, up_weight, down_weight, expert_ids, gate_values):
    rows, width = state.shape[2], state.shape[3]
    hidden = up_weight.shape[4]
    chips = experts // 2
    routes = jnp.transpose(expert_ids[:, :, 0], (2, 0, 1, 3)).reshape(experts * rows, tick_count * 4)
    gates = jnp.transpose(gate_values[:, :, 0], (1 + 1, 0, 1, 3)).reshape(rows, tick_count * 4)
    routes = jnp.pad(routes, ((0, 0), (0, LANES - tick_count * 4)))
    gates = jnp.pad(gates, ((0, 0), (0, LANES - tick_count * 4)))
    vmem = pl.BlockSpec(memory_space=pltpu.VMEM)
    hbm = pl.BlockSpec(memory_space=pl.ANY)
    bf16 = jnp.bfloat16
    dma = pltpu.SemaphoreType.DMA
    final, finished = pl.pallas_call(
        functools.partial(relay_kernel, tick_count, chips, sections, rows, tile),
        out_shape=(
            jax.ShapeDtypeStruct((2, rows, width), bf16),
            jax.ShapeDtypeStruct((tick_count, rows, width // sections), bf16),
        ),
        in_specs=[vmem, vmem, hbm, hbm, vmem, vmem],
        out_specs=(vmem, vmem),
        scratch_shapes=[
            pltpu.VMEM((2, width, hidden), bf16),
            pltpu.VMEM((2, hidden, width), bf16),
            pltpu.VMEM((tick_count + 1, 2, rows, width), bf16),
            pltpu.VMEM((2, experts * rows, width), bf16),
            pltpu.VMEM((2, experts * rows, width), bf16),
            pltpu.VMEM((2, chips * rows, width), bf16),
            pltpu.VMEM((2, 2, chips * rows, width), bf16),
            pltpu.VMEM((2, rows, width), bf16),
            pltpu.VMEM((experts * rows, hidden), bf16),
            pltpu.VMEM((experts * rows, tile), jnp.float32),
            pltpu.VMEM((experts * rows, LANES), jnp.float32),
            dma((4,)), dma((experts,)), dma((experts,)),
            dma((2, 2, chips, 4)), dma((2, chips, 4)), dma((2, chips)), dma((2, chips)),
            dma((2, chips)), dma((2, chips)), dma((2, chips, 4)), dma((2, 2, chips, 4)),
            dma((2, 4)), dma((tick_count, 2, 4)), dma((sections,)), dma((tick_count,)), dma(()),
        ],
        compiler_params=pltpu.CompilerParams(
            collective_id=0, has_side_effects=True, vmem_limit_bytes=VMEM_LIMIT),
        cost_estimate=pl.CostEstimate(
            flops=tick_count * 2 * experts * rows * width * hidden * 4,
            bytes_accessed=8 * width * hidden, transcendentals=0),
    )(state[:, 0], norm_gain[:, 0], up_weight[:, 0, 0], down_weight[:, 0, 0], routes, gates)
    return final[:, None], finished


def from_behind(block, axis, distance):
    devices = range(lax.axis_size(axis))
    route = [((i - distance) % len(devices), i) for i in devices]
    return lax.ppermute(block, axis, route)


def spread(value, axis, root):
    mine = lax.axis_index(axis) == root
    return lax.psum(jnp.where(mine, value, jnp.zeros_like(value)), axis)


def rms_norm(layer_in, norm_gain):
    widened = layer_in.astype(jnp.float32)
    scaled = lax.rsqrt(jnp.mean(widened * widened, axis=-1, keepdims=True) + 1e-06)
    return (widened * scaled * norm_gain).astype(jnp.bfloat16)


def expert_mlp(in_rows, up_weight, down_weight):
    projected = jnp.einsum("srd,sdf->srf", in_rows, up_weight, preferred_element_type=jnp.float32)
    activated = jax.nn.silu(projected).astype(jnp.bfloat16)
    return jnp.einsum(
        "srf,sfd->srd", activated, down_weight, preferred_element_type=jnp.float32
    ).astype(jnp.bfloat16)


def source_bound(tok_rows, expert_count):
    return max(2, 4 * tok_rows // expert_count)


def through_exchange(layer_in, normed, up_weight, down_weight, routes, gates, expert_count, owner):
    slot_count, tok_rows, model_width = layer_in.shape
    per_source = source_bound(tok_rows, expert_count)
    own_routes = lax.dynamic_slice_in_dim(routes, owner * tok_rows, tok_rows, 1)
    matches = (own_routes[..., None] == jnp.arange(expert_count, dtype=jnp.int32)).astype(jnp.int32)
    flattened = matches.reshape(slot_count, tok_rows * 2, expert_count)
    picks = jnp.arange(tok_rows * 2)
    before = (picks[:, None] > picks[None, :]).astype(jnp.bfloat16)
    earlier = jnp.einsum(
        "ab,sbe->sae", before, flattened.astype(jnp.bfloat16), preferred_element_type=jnp.float32
    )
    earlier = earlier.astype(jnp.int32).reshape(slot_count, tok_rows, 2, expert_count)
    position = jnp.sum(earlier * matches, axis=3)
    slot_match = (position[..., None, None] == jnp.arange(per_source, dtype=jnp.int32)).astype(
        jnp.int32
    )
    chosen = matches[..., None] * slot_match
    dispatch = jnp.sum(chosen, axis=2).astype(jnp.bfloat16)
    weights = jnp.sum(chosen.astype(jnp.float32) * gates[..., None, None], axis=2)
    outgoing = jnp.einsum(
        "stjp,std->sjpd", dispatch, normed, preferred_element_type=jnp.float32
    ).astype(jnp.bfloat16)
    in_rows = lax.all_to_all(outgoing, "expert", split_axis=1, concat_axis=1, tiled=True)
    shaped = in_rows.reshape(slot_count, -1, model_width)
    outputs = expert_mlp(shaped, up_weight, down_weight).reshape(in_rows.shape)
    returned = lax.all_to_all(outputs, "expert", split_axis=1, concat_axis=1, tiled=True)
    combined = jnp.einsum(
        "stjp,sjpd->std", weights, returned.astype(jnp.float32), precision=lax.Precision.HIGHEST
    )
    return (layer_in.astype(jnp.float32) + combined).astype(jnp.bfloat16)


def advance(layer_in, norm_gain, up_weight, down_weight, routes, gates, expert_count, owner):
    normed = rms_norm(layer_in, norm_gain[:, None, :])
    return through_exchange(
        layer_in, normed, up_weight, down_weight, routes, gates, expert_count, owner
    )


def on_device(state, norm_gain, up_weight, down_weight, expert_ids, gate_values):
    expert_count = lax.axis_size("expert")
    segment_count = lax.axis_size("section")
    owner = lax.axis_index("expert")
    segment_place = lax.axis_index("section")
    gains = norm_gain[:, 0]
    up_local = up_weight[:, 0, 0]
    down_local = down_weight[:, 0, 0]
    current = state[:, 0]
    done_list = []
    for tick_index in range(expert_ids.shape[0]):
        routes = expert_ids[tick_index, :, 0]
        gates = gate_values[tick_index, :, 0]
        stepped = advance(current, gains, up_local, down_local, routes, gates, expert_count, owner)
        arrived = from_behind(stepped, "section", 1)
        at_start = segment_place == 0
        new_first = jnp.where(at_start, jnp.zeros_like(arrived[0]), arrived[0])
        new_second = jnp.where(at_start, arrived[0], arrived[1])
        done_list.append(arrived[1])
        current = jnp.stack([new_first, new_second])
    leaving = jnp.stack(done_list)
    leaving = spread(leaving, "section", 0)
    columns = leaving.shape[2] // segment_count
    finished = lax.dynamic_slice_in_dim(leaving, segment_place * columns, columns, 2)
    return (current[:, None], finished)


def solution(mesh):
    experts, sections = mesh.shape["expert"], mesh.shape["section"]

    def whole(state, norm_gain, up_weight, down_weight, expert_ids, gate_values):
        ticks = expert_ids.shape[0]
        rows, width, hidden = state.shape[2] // experts, state.shape[3], up_weight.shape[4]
        tile = tile_of(width, hidden)
        fits = (
            experts % 2 == 0 and experts >= 4 and sections >= 2 and rows % 16 == 0 and tile
            and width % (sections * LANES) == 0 and ticks * 4 <= LANES
            and relay_bytes(ticks, experts, rows, width, hidden) <= VMEM_BUDGET
        )
        body = on_device
        if fits:
            body = functools.partial(on_device_relay, ticks, experts, sections, tile)
        return jax.shard_map(
            body,
            mesh=mesh,
            in_specs=(
                P(None, "section", "expert", None),
                P(None, "section", None),
                P(None, "section", "expert", None, None),
                P(None, "section", "expert", None, None),
                P(None, None, "section", None, None),
                P(None, None, "section", "expert", None),
            ),
            out_specs=(P(None, "section", "expert", None), P(None, "expert", "section")),
            check_vma=False,
        )(state, norm_gain, up_weight, down_weight, expert_ids, gate_values)

    return whole
```
